128 devices in a mesh: seq: 16 (over z, y), head: 8 (over x, core).
Axes of the slice: x: 4, y: 4, z: 4, core: 2. Of those that a mesh axis runs over, the one named last changes fastest.
Arguments:
- queries: bfloat16 [16384, 4096], P(('seq', 'head')), may hold values from -6 to 6
- keys: bfloat16 [16384, 2, 4096], P(('seq', 'head')), may hold values from -6 to 6
- values: bfloat16 [16384, 2, 4096], P(('seq', 'head')), may hold values from -6 to 6
- betas: bfloat16 [16384, 2, 16], P(('seq', 'head')), may hold values from 0.2 to 2, as said below
- gate: bfloat16 [16384, 4096], P(('seq', 'head')), may hold values from -6 to 6
- norm_gain: float32 [256], replicated, may hold values from 0.1 to 1.9
Outputs:
- mixed: bfloat16 [16384, 4096], P(('seq', 'head'))
The draws below stay inside these ranges and needn't reach their ends.
Inputs may be any that keep to these rules, and one draw needn't show every extreme that they name: `betas`: each entry is the step size of one reflection of one head.
All inputs are finite; a program needn't handle non-finite values.
Results may differ from the reference program's by a relative error of at most 0.0049.
Values may be sent and summed in bfloat16 or wider, within the bound.
A program may use at most 128 MiB of HBM per device.

```python
import jax
import jax.numpy as jnp
from jax import lax

H = 16
DK = 256
REFL = 2
CT = 128
STREAM_LENGTH = 16384


def draw_betas(key, part):
    first_key, second_key, third_key, mirror_direction_last = jax.random.split(jax.random.fold_in(key, 17), 4)
    slow_share = 0.5
    slow_heads = jax.random.uniform(first_key, (H,)) < slow_share
    slow_forget_factors = jax.random.uniform(second_key, (STREAM_LENGTH, REFL, H), minval=1.996, maxval=2.0)
    quick_decay_rates = jax.random.uniform(third_key, (STREAM_LENGTH, REFL, H), minval=0.2, maxval=1.8)
    segment_groups = jax.random.uniform(mirror_direction_last, (STREAM_LENGTH, 1, 1)) < 8.0 / STREAM_LENGTH
    slow_payload_vectors = jnp.where(segment_groups, 1.0, slow_forget_factors)
    rates = jnp.where(slow_heads[None, None, :], slow_payload_vectors, quick_decay_rates)
    return rates.astype(jnp.bfloat16)


def level_of(rng, dims, cuts, low, high):
    gain = 1.0
    for dim, blocks in cuts:
        draws = jax.random.uniform(jax.random.fold_in(jax.random.fold_in(rng, 6), dim), (blocks,), jnp.float32, low / len(cuts), high / len(cuts))
        gain = gain * jnp.repeat(jnp.exp(draws), dims[dim] // blocks).reshape((-1,) + (1,) * (len(dims) - 1 - dim))
    return gain


def normal_values(stream_key, extent, spread, limit, cuts=(), kind=jnp.bfloat16):
    factor_of = level_of(stream_key, extent, cuts, -0.22, 0.18) if cuts else 1.0
    result = jax.random.normal(stream_key, extent, jnp.float32) * spread * factor_of
    return jnp.minimum(jnp.maximum(result, -limit), limit).astype(kind)


def setup_inputs(seed: int = 0) -> dict:
    arg_keys = jax.random.split(jax.random.key(seed), 7)
    queries = normal_values(arg_keys[0], (STREAM_LENGTH, H * DK), 1.0, 6.0, ((0, 128),))
    keys = normal_values(arg_keys[1], (STREAM_LENGTH, REFL, H * DK), 1.0, 6.0, ((0, 128),))
    values = normal_values(arg_keys[2], (STREAM_LENGTH, REFL, H * DK), 1.0, 6.0, ((0, 128),))
    betas = draw_betas(jax.random.fold_in(arg_keys[6], 71), 0)
    gate = normal_values(arg_keys[4], (STREAM_LENGTH, H * DK), 1.0, 6.0, ((0, 128),))
    norm_gain = jnp.clip(1.0 + 0.18 * jax.random.normal(arg_keys[5], (DK,), jnp.float32), 0.1, 1.9)
    return {"queries": queries, "keys": keys, "values": values, "betas": betas, "gate": gate, "norm_gain": norm_gain}


epsilon = 1e-06
highest = lax.Precision.HIGHEST

def unit_rows(matrix):
    return matrix / jnp.sqrt(lax.optimization_barrier(jnp.sum(matrix * matrix, axis=-1, keepdims=True)) + epsilon)

def block_mask(block_tokens, reflections):
    step_iota = lax.broadcasted_iota(jnp.int32, (block_tokens, block_tokens * reflections), 1)
    token_iota = lax.broadcasted_iota(jnp.int32, (block_tokens, block_tokens * reflections), 0)
    return step_iota // reflections <= token_iota

def head_pass(input_arrays):
    query_rows, key_rows, value_rows, beta_rows = input_arrays
    row_count = query_rows.shape[0]
    width_per_head = query_rows.shape[-1]
    blocks = row_count // CT
    block_steps = CT * REFL
    query_blocks = unit_rows(query_rows.astype(jnp.float32)).reshape(blocks, CT, width_per_head)
    k_blocks = unit_rows(key_rows.astype(jnp.float32)).reshape(blocks, block_steps, width_per_head)
    v_blocks = value_rows.astype(jnp.float32).reshape(blocks, block_steps, width_per_head)
    b_blocks = beta_rows.astype(jnp.float32).reshape(blocks, block_steps)
    causal = block_mask(CT, REFL)

    def advance(carried, pieces):
        q_now, k_now, v_now, b_now = pieces
        gram_rows = jnp.dot(k_now, k_now.T, precision=highest)
        lower_part = jnp.tril(gram_rows, -1) * b_now[None, :]
        solved = lax.linalg.triangular_solve(lower_part, jnp.concatenate([k_now, v_now], axis=1), left_side=True, lower=True, unit_diagonal=True)
        w_rows = solved[:, :width_per_head] * b_now[:, None]
        y_rows = solved[:, width_per_head:] * b_now[:, None]
        update_rows = y_rows - jnp.dot(w_rows, carried, precision=highest)
        scores = jnp.where(causal, jnp.dot(q_now, k_now.T, precision=highest), jnp.zeros((), jnp.float32))
        output = jnp.dot(q_now, carried, precision=highest) + jnp.dot(scores, update_rows, precision=highest)
        carried = carried + jnp.dot(k_now.T, update_rows, precision=highest)
        return (carried, output)
    start = jnp.zeros((width_per_head, width_per_head), jnp.float32)
    final_state, outputs = lax.scan(advance, start, (query_blocks, k_blocks, v_blocks, b_blocks))
    return outputs.reshape(row_count, width_per_head)

def reference(queries, keys, values, betas, gate, norm_gain):
    row_count = queries.shape[0]
    width_per_head = norm_gain.shape[0]
    head_count = queries.shape[1] // width_per_head
    q_heads = queries.reshape(row_count, head_count, width_per_head).transpose(1, 0, 2)
    k_heads = keys.reshape(row_count, REFL, head_count, width_per_head).transpose(2, 0, 1, 3)
    v_heads = values.reshape(row_count, REFL, head_count, width_per_head).transpose(2, 0, 1, 3)
    b_heads = betas.transpose(2, 0, 1)
    outputs = lax.map(head_pass, (q_heads, k_heads, v_heads, b_heads)).transpose(1, 0, 2)
    normed = outputs * lax.rsqrt(lax.optimization_barrier(jnp.mean(outputs * outputs, axis=-1, keepdims=True)) + epsilon) * norm_gain
    normed = lax.optimization_barrier(normed.astype(jnp.bfloat16))
    gated = normed.astype(jnp.float32).reshape(row_count, head_count * width_per_head) * jax.nn.silu(gate.astype(jnp.float32))
    return gated.astype(jnp.bfloat16)
```

```python
import functools

import jax
import jax.numpy as jnp
from jax import lax
from jax.experimental import pallas as pl
from jax.experimental.pallas import tpu as pltpu
from jax.sharding import Mesh
from jax.sharding import PartitionSpec as P

H = 16
DK = 256
CT = 128
STEPS = 256
EPS = 1e-06
LEVELS = 8
PER = 2
f32 = jnp.float32
bf16 = jnp.bfloat16
AXES = ("z", "y", "x", "core")
highest = lax.Precision.HIGHEST


def mm(a, b, dims=((1,), (0,))):
    return lax.dot_general(a, b, (dims, ((), ())), preferred_element_type=f32)


def split(x):
    hi = x.astype(bf16)
    return hi, (x - hi.astype(f32)).astype(bf16)


def mm_right(a, b):
    hi, lo = b
    return mm(a, hi) + mm(a, lo)


def mm_both(a, b):
    return mm(a[0], b[0]) + (mm(a[0], b[1]) + mm(a[1], b[0]))


def factors(k, v, q, beta_row, mask_ref):
    row = lax.broadcasted_iota(jnp.int32, (STEPS, STEPS), 0)
    col = lax.broadcasted_iota(jnp.int32, (STEPS, STEPS), 1)
    eye = row == col
    gram = mm(k, k, ((1,), (1,)))
    g = jnp.sum(jnp.where(eye, gram, 0.0), axis=0, keepdims=True) + EPS
    c = beta_row / g
    lower = jnp.where(row > col, gram, 0.0)
    low = split(lower)
    tau = jnp.where(eye, c, 0.0)
    for level in range(LEVELS):
        edge = low[0] * mask_ref[level]
        tb = tau.astype(bf16)
        step = (edge.astype(f32) * c if level == 0 else mm(edge, tb)).astype(bf16)
        tau = tau - mm(tb, step)
    tb = tau.astype(bf16)
    t32 = tb.astype(f32)
    rest = jnp.where(eye, 1.0, 0.0) - t32 * (g / beta_row) - mm_right(tb, low)
    tau = t32 + mm(rest.astype(bf16), tb)
    ts = split(tau)
    w = split(mm(ts[0], k) + mm(ts[1], k))
    ts = split(tau * jnp.sqrt(g))
    y = split(mm(ts[0], v) + mm(ts[1], v))
    kt = k.T
    a = jnp.where(eye, 1.0, 0.0) - mm_right(kt, w)
    b = mm_right(kt, y)
    token = lax.broadcasted_iota(jnp.int32, (CT, STEPS), 0)
    step_of = lax.broadcasted_iota(jnp.int32, (CT, STEPS), 1)
    p = split(jnp.where(step_of // 2 <= token, mm(q, k, ((1,), (1,))), 0.0))
    q32 = q.astype(f32)
    unit = lax.rsqrt(jnp.sum(q32 * q32, axis=-1, keepdims=True) + EPS)
    qt = (q32 - mm_both(p, w)) * unit
    ot = mm_both(p, y) * unit
    return a, b, qt, ot


def make_masks(mask_ref):
    row = lax.broadcasted_iota(jnp.int32, (STEPS, STEPS), 0)
    col = lax.broadcasted_iota(jnp.int32, (STEPS, STEPS), 1)
    differ = jnp.bitwise_xor(row, col)
    for level in range(LEVELS):
        inside = (differ >= (1 << level)) & (differ < (2 << level))
        mask_ref[level] = jnp.where(inside, 1.0, 0.0).astype(bf16)


def local_kernel(q_ref, k_ref, v_ref, beta_ref, a_ref, b_ref, qt_ref, ot_ref, mask_ref):
    @pl.when(pl.program_id(0) == 0)
    def _():
        make_masks(mask_ref)

    for i in range(PER):
        lanes = slice(i * DK, (i + 1) * DK)
        k = k_ref[:, :, lanes].reshape(STEPS, DK)
        v = v_ref[:, :, lanes].reshape(STEPS, DK)
        a, b, qt, ot = factors(k, v, q_ref[:, lanes], beta_ref[i], mask_ref)
        a_ref[i] = a
        b_ref[i] = b
        qt_ref[i] = qt
        ot_ref[i] = ot


def local_factors(queries, keys, values, beta_rows):
    tokens = pl.BlockSpec((CT, PER * DK), lambda i: (0, i))
    pairs = pl.BlockSpec((CT, 2, PER * DK), lambda i: (0, 0, i))
    square = pl.BlockSpec((PER, DK, DK), lambda i: (i, 0, 0))
    half = pl.BlockSpec((PER, CT, DK), lambda i: (i, 0, 0))
    return pl.pallas_call(
        local_kernel,
        grid=(H // PER,),
        in_specs=[tokens, pairs, pairs, pl.BlockSpec((PER, 1, STEPS), lambda i: (i, 0, 0))],
        out_specs=[square, square, half, half],
        out_shape=[jax.ShapeDtypeStruct((H, DK, DK), f32)] * 2
        + [jax.ShapeDtypeStruct((H, CT, DK), f32)] * 2,
        scratch_shapes=[pltpu.VMEM((LEVELS, STEPS, STEPS), bf16)],
        compiler_params=pltpu.CompilerParams(vmem_limit_bytes=48 << 20),
    )(queries, keys, values, beta_rows)


def gated(o, gain, gate):
    scale = lax.rsqrt(jnp.mean(o * o, axis=-1, keepdims=True) + EPS)
    normed = (o * scale * gain).astype(bf16).astype(f32)
    gate = gate.astype(f32)
    return (normed * (gate / (1.0 + jnp.exp(-gate)))).astype(bf16)


def output_kernel(s_ref, qt_ref, ot_ref, gate_ref, gain_ref, out_ref):
    for i in range(PER):
        lanes = slice(i * DK, (i + 1) * DK)
        o = mm_both(split(qt_ref[i]), split(s_ref[i])) + ot_ref[i]
        out_ref[:, lanes] = gated(o, gain_ref[...], gate_ref[:, lanes])


def outputs(state, qt, ot, gate, gain):
    tokens = pl.BlockSpec((CT, PER * DK), lambda i: (0, i))
    square = pl.BlockSpec((PER, DK, DK), lambda i: (i, 0, 0))
    half = pl.BlockSpec((PER, CT, DK), lambda i: (i, 0, 0))
    return pl.pallas_call(
        output_kernel,
        grid=(H // PER,),
        in_specs=[square, half, half, tokens, pl.BlockSpec((1, DK), lambda i: (0, 0))],
        out_specs=tokens,
        out_shape=jax.ShapeDtypeStruct((CT, H * DK), bf16),
        compiler_params=pltpu.CompilerParams(vmem_limit_bytes=48 << 20),
    )(state, qt, ot, gate, gain)


def einmul(a, b):
    return jnp.einsum("hde,hef->hdf", a, b, precision=highest)


def prefixes(a, b):
    pairs = [(a[0], b[0])]
    for i in range(1, a.shape[0]):
        pairs.append((einmul(a[i], pairs[-1][0]), einmul(a[i], pairs[-1][1]) + b[i]))
    return pairs


def entering(start, pairs, index, stack=False):
    states = [start] + [einmul(p[0], start) + p[1] for p in pairs[:-1]]
    states = jnp.stack(states)
    if stack:
        return states
    return lax.dynamic_index_in_dim(states, index, 0, keepdims=False)


def shards(queries, keys, values, betas, gate, norm_gain):
    beta_rows = betas.astype(f32).transpose(2, 0, 1).reshape(H, 1, STEPS)
    a, b, qt, ot = local_factors(queries, keys, values, beta_rows)
    ab = jnp.concatenate([a, b], axis=-1).reshape(2, 4, 2, DK, 2 * DK)
    ab = lax.all_to_all(ab, "core", 0, 0, tiled=True)
    own = [(ab[i, ..., :DK].reshape(8, DK, DK), ab[i, ..., DK:].reshape(8, DK, DK)) for i in (0, 1)]
    chip_a = einmul(own[1][0], own[0][0])
    chip_b = einmul(own[1][0], own[0][1]) + own[1][1]
    ab = jnp.concatenate([chip_a, chip_b], axis=-1).reshape(4, 2, DK, 2 * DK)
    ab = lax.all_to_all(ab, "x", 0, 0, tiled=True)
    in_x = prefixes(ab[..., :DK], ab[..., DK:])
    ab = lax.all_gather(jnp.concatenate(in_x[-1], axis=-1), "y")
    in_y = prefixes(ab[..., :DK], ab[..., DK:])
    ab = lax.all_gather(jnp.concatenate(in_y[-1], axis=-1), "z")
    in_z = [(ab[i, ..., :DK], ab[i, ..., DK:]) for i in range(4)]
    state = jnp.zeros((2, DK, DK), f32)
    states = [state]
    for i in range(3):
        state = einmul(in_z[i][0], state) + in_z[i][1]
        states.append(state)
    state = lax.dynamic_index_in_dim(jnp.stack(states), lax.axis_index("z"), 0, keepdims=False)
    state = entering(state, in_y, lax.axis_index("y"))
    states = entering(state, in_x, 0, stack=True)
    states = lax.all_to_all(states, "x", 0, 0, tiled=True).reshape(8, DK, DK)
    later = einmul(own[0][0], states) + own[0][1]
    states = lax.all_to_all(jnp.stack([states, later]), "core", 0, 0, tiled=True)
    return outputs(states.reshape(H, DK, DK), qt, ot, gate, norm_gain.reshape(1, DK))


def solution(mesh):
    torus = Mesh(mesh.devices.reshape(4, 4, 4, 2), AXES)
    placed = (P(AXES, None), P(AXES, None, None), P(AXES, None, None), P(AXES, None, None), P(AXES, None), P())
    return jax.shard_map(
        shards, mesh=torus, in_specs=placed, out_specs=P(AXES, None), check_vma=False
    )
```

```python
import functools

import jax
import jax.numpy as jnp
from jax import lax
from jax.experimental import pallas as pl
from jax.experimental.pallas import tpu as pltpu
from jax.sharding import Mesh
from jax.sharding import PartitionSpec as P

H = 16
DK = 256
CT = 128
STEPS = 256
EPS = 1e-06
LEVELS = 8
f32 = jnp.float32
bf16 = jnp.bfloat16
AXES = ("z", "y", "x", "core")
MESH = pl.DeviceIdType.MESH


def mm(a, b, dims=((1,), (0,))):
    return lax.dot_general(a, b, (dims, ((), ())), preferred_element_type=f32)


def split(x):
    hi = x.astype(bf16)
    return hi, (x - hi.astype(f32)).astype(bf16)


def mm_right(a, b):
    hi, lo = b
    return mm(a, hi) + mm(a, lo)


def mm_both(a, b):
    return mm(a[0], b[0]) + (mm(a[0], b[1]) + mm(a[1], b[0]))


def factors(ks, vs, qs, beta_rows, mask_ref):
    row = lax.broadcasted_iota(jnp.int32, (STEPS, STEPS), 0)
    col = lax.broadcasted_iota(jnp.int32, (STEPS, STEPS), 1)
    eye = row == col
    n = range(len(ks))
    gram = [mm(k, k, ((1,), (1,))) for k in ks]
    g = [jnp.sum(jnp.where(eye, x, 0.0), axis=0, keepdims=True) + EPS for x in gram]
    c = [beta_rows[i] / g[i] for i in n]
    low = [split(jnp.where(row > col, x, 0.0)) for x in gram]
    tau = [jnp.where(eye, x, 0.0) for x in c]
    for level in range(LEVELS):
        edge = [x[0] * mask_ref[level] for x in low]
        tb = [x.astype(bf16) for x in tau]
        if level == 0:
            step = [(edge[i].astype(f32) * c[i]).astype(bf16) for i in n]
        else:
            step = [mm(edge[i], tb[i]).astype(bf16) for i in n]
        tau = [tau[i] - mm(tb[i], step[i]) for i in n]
    tb = [x.astype(bf16) for x in tau]
    t32 = [x.astype(f32) for x in tb]
    rest = [
        jnp.where(eye, 1.0, 0.0) - t32[i] * (g[i] / beta_rows[i]) - mm_right(tb[i], low[i]) for i in n
    ]
    tau = [t32[i] + mm(rest[i].astype(bf16), tb[i]) for i in n]
    ts = [split(x) for x in tau]
    w = [split(mm(ts[i][0], ks[i]) + mm(ts[i][1], ks[i])) for i in n]
    ts = [split(tau[i] * jnp.sqrt(g[i])) for i in n]
    y = [split(mm(ts[i][0], vs[i]) + mm(ts[i][1], vs[i])) for i in n]
    kt = [k.T for k in ks]
    a = [jnp.where(eye, 1.0, 0.0) - mm_right(kt[i], w[i]) for i in n]
    b = [mm_right(kt[i], y[i]) for i in n]
    token = lax.broadcasted_iota(jnp.int32, (CT, STEPS), 0)
    step_of = lax.broadcasted_iota(jnp.int32, (CT, STEPS), 1)
    causal = step_of // 2 <= token
    p = [split(jnp.where(causal, mm(qs[i], ks[i], ((1,), (1,))), 0.0)) for i in n]
    q32 = [q.astype(f32) for q in qs]
    unit = [lax.rsqrt(jnp.sum(q * q, axis=-1, keepdims=True) + EPS) for q in q32]
    qt = [(q32[i] - mm_both(p[i], w[i])) * unit[i] for i in n]
    ot = [mm_both(p[i], y[i]) * unit[i] for i in n]
    return a, b, qt, ot


def make_masks(mask_ref):
    row = lax.broadcasted_iota(jnp.int32, (STEPS, STEPS), 0)
    col = lax.broadcasted_iota(jnp.int32, (STEPS, STEPS), 1)
    differ = jnp.bitwise_xor(row, col)
    for level in range(LEVELS):
        inside = (differ >= (1 << level)) & (differ < (2 << level))
        mask_ref[level] = jnp.where(inside, 1.0, 0.0).astype(bf16)


def gated(o, gain, gate):
    scale = lax.rsqrt(jnp.mean(o * o, axis=-1, keepdims=True) + EPS)
    normed = (o * scale * gain).astype(bf16).astype(f32)
    gate = gate.astype(f32)
    return (normed * (gate / (1.0 + jnp.exp(-gate)))).astype(bf16)


def put_pair(ref, values):
    ref[0], ref[1] = split(values)


def layer_kernel(
    q_ref, k_ref, v_ref, beta_ref, gate_ref, gain_ref, out_ref,
    mask, qt, ot, blk, x_out, x_in, pxa, pxb, y_in, pya, pyb, line_a, line_b, z_in, z_out,
    s_out, s_in, mine, c_out, c_in,
    core_send, core_recv, x_send, x_recv, y_send, y_recv, z_send, z_recv, s_send, s_recv,
    c_send, c_recv, here,
):
    z, y, x, c = (lax.axis_index(name) for name in AXES)
    other = {"core": 1 - c}

    def along(axis, index, offset):
        return {axis: lax.rem(index + offset, 4)}

    barrier = pltpu.get_barrier_semaphore()
    greeted = [other] + [along("x", x, o) for o in (1, 2, 3)] + [along("y", y, o) for o in (1, 2, 3)]
    greeted += [along("z", z, o) for o in (1, 3)]
    for device in greeted:
        pl.semaphore_signal(barrier, inc=1, device_id=device, device_id_type=MESH)

    def remote(src, dst, send, recv, device):
        return pltpu.make_async_remote_copy(
            src_ref=src, dst_ref=dst, send_sem=send, recv_sem=recv, device_id=device, device_id_type=MESH
        )

    def core_copy(j, slot):
        return remote(blk.at[2, j], blk.at[slot, j], core_send.at[j], core_recv.at[j], other)

    def x_copy(i, o, j, source):
        return remote(
            x_out.at[j], x_in.at[source, i], x_send.at[o, i], x_recv.at[source, i], along("x", x, o)
        )

    def y_copy(i, o, source):
        return remote(
            y_in.at[y, i], y_in.at[source, i], y_send.at[o, i], y_recv.at[source, i], along("y", y, o)
        )

    def z_copy(i):
        return remote(z_out.at[i], z_in.at[i], z_send.at[i], z_recv.at[i], along("z", z, 1))

    def s_copy(i, o, dest, source):
        j = 2 * source + i
        return remote(s_out.at[dest, i], s_in.at[j], s_send.at[o, i], s_recv.at[j], along("x", x, o))

    def c_copy(j):
        return remote(c_out.at[j], c_in.at[j], c_send.at[j], c_recv.at[j], other)

    def lanes_of(head):
        return pl.ds(pl.multiple_of(head * DK, DK), DK)

    make_masks(mask)

    def phase(p, carry):
        i, own = p // 2, p % 2
        group = own * c + (1 - own) * (1 - c)
        slot = own * c + (1 - own) * 2
        heads = [8 * group + 2 * n + i for n in range(4)]
        lanes = [lanes_of(h) for h in heads]
        a, b, q_now, o_now = factors(
            [k_ref[:, :, n].reshape(STEPS, DK) for n in lanes],
            [v_ref[:, :, n].reshape(STEPS, DK) for n in lanes],
            [q_ref[:, n] for n in lanes],
            [beta_ref[h] for h in heads],
            mask,
        )
        for n in range(4):
            j = 2 * n + i
            put_pair(blk.at[slot, j, pl.ds(0, 2)], a[n])
            put_pair(blk.at[slot, j, pl.ds(2, 2)], b[n])
            qt[heads[n]] = q_now[n]
            ot[heads[n]] = o_now[n]

        @pl.when(p == 0)
        def _():
            pl.semaphore_wait(barrier, len(greeted))

        @pl.when(own == 0)
        def _():
            for n in range(4):
                core_copy(2 * n + i, c).start()

        @pl.when(own == 1)
        def _():
            for o in (1, 3, 2, 0):
                dest = lax.rem(x + o, 4)
                j = 2 * dest + i
                core_copy(j, 1 - c).wait_recv()
                later = (blk[1, j, 0], blk[1, j, 1])
                put_pair(x_out.at[j, pl.ds(0, 2)], mm_both(later, (blk[0, j, 0], blk[0, j, 1])))
                x_out[j, 2] = (
                    mm_both(later, (blk[0, j, 2], blk[0, j, 3]))
                    + blk[1, j, 2].astype(f32)
                    + blk[1, j, 3].astype(f32)
                ).astype(bf16)
                if o:
                    x_copy(i, o, j, x).start()
                else:
                    pltpu.make_async_copy(x_out.at[j], x_in.at[x, i], here.at[i]).start()

        return carry

    lax.fori_loop(0, 4, phase, 0)

    def compose(pairs, i, pa, pb):
        eye = lax.broadcasted_iota(jnp.int32, (DK, DK), 0) == lax.broadcasted_iota(jnp.int32, (DK, DK), 1)
        pa[i, 0, 0] = jnp.where(eye, 1.0, 0.0).astype(bf16)
        pa[i, 0, 1] = jnp.zeros((DK, DK), bf16)
        pb[i, 0] = jnp.zeros((DK, DK), f32)
        a = (pairs[0, i, 0], pairs[0, i, 1])
        b = pairs[0, i, 2].astype(f32)
        for n in range(1, 4):
            pa[i, n, 0], pa[i, n, 1] = a
            pb[i, n] = b
            later = (pairs[n, i, 0], pairs[n, i, 1])
            a = split(mm_both(later, a))
            b = mm_both(later, split(b)) + pairs[n, i, 2].astype(f32)
        return a, b

    def over_x(i, carry):
        pltpu.make_async_copy(x_out.at[2 * x + i], x_in.at[x, i], here.at[i]).wait()
        for o in (1, 3, 2):
            source = lax.rem(x + o, 4)
            x_copy(i, o, 2 * source + i, source).wait_recv()
        a, b = compose(x_in, i, pxa, pxb)
        y_in[y, i, 0], y_in[y, i, 1] = a
        y_in[y, i, 2] = b.astype(bf16)
        for o in (1, 3, 2):
            y_copy(i, o, y).start()
        return carry

    lax.fori_loop(0, 2, over_x, 0)

    def over_y(i, carry):
        for o in (1, 3, 2):
            y_copy(i, o, lax.rem(y + o, 4)).wait_recv()
        a, b = compose(y_in, i, pya, pyb)
        line_a[i, 0], line_a[i, 1] = a
        line_b[i] = b

        @pl.when(z == 0)
        def _():
            z_in[i] = jnp.zeros((DK, DK), bf16)

        @pl.when(z > 0)
        def _():
            z_copy(i).wait_recv()

        @pl.when(z < 3)
        def _():
            s = z_in[i]
            z_out[i] = (mm(line_a[i, 0], s) + mm(line_a[i, 1], s) + line_b[i]).astype(bf16)
            z_copy(i).start()

        s = z_in[i]
        s = split(mm(pya[i, y, 0], s) + mm(pya[i, y, 1], s) + pyb[i, y])
        for o in (1, 3, 2, 0):
            dest = lax.rem(x + o, 4)
            now = (mm_both((pxa[i, dest, 0], pxa[i, dest, 1]), s) + pxb[i, dest]).astype(bf16)
            if o:
                s_out[dest, i] = now
                s_copy(i, o, dest, x).start()
            else:
                s_in[2 * x + i] = now
        return carry

    lax.fori_loop(0, 2, over_y, 0)

    def over_cores(i, carry):
        for o in (0, 1, 3, 2):
            source = lax.rem(x + o, 4)
            j = 2 * source + i
            if o:
                s_copy(i, o, source, source).wait_recv()
            first = s_in[j]
            second = (
                mm(blk[0, j, 0], first)
                + mm(blk[0, j, 1], first)
                + blk[0, j, 2].astype(f32)
                + blk[0, j, 3].astype(f32)
            ).astype(bf16)
            mine[j] = jnp.where(c == 0, first, second)
            c_out[j] = jnp.where(c == 0, second, first)
            c_copy(j).start()
        return carry

    lax.fori_loop(0, 2, over_cores, 0)

    def finish(head, state):
        q_now = split(qt[head])
        o = mm(q_now[0], state) + mm(q_now[1], state) + ot[head]
        lanes = lanes_of(head)
        out_ref[:, lanes] = gated(o, gain_ref[...], gate_ref[:, lanes])

    def last_own(j, carry):
        finish(8 * c + j, mine[j])
        return carry

    def last_other(j, carry):
        c_copy(j).wait_recv()
        finish(8 * (1 - c) + j, c_in[j])
        return carry

    lax.fori_loop(0, 8, last_own, 0)
    lax.fori_loop(0, 8, last_other, 0)

    def drain(j, carry):
        core_copy(j, c).wait_send()
        c_copy(j).wait_send()
        return carry

    def drain_links(i, carry):
        for o in (1, 2, 3):
            dest = lax.rem(x + o, 4)
            x_copy(i, o, 2 * dest + i, x).wait_send()
            y_copy(i, o, y).wait_send()
            s_copy(i, o, dest, x).wait_send()

        @pl.when(z < 3)
        def _():
            z_copy(i).wait_send()

        return carry

    lax.fori_loop(0, 8, drain, 0)
    lax.fori_loop(0, 2, drain_links, 0)


def shards(queries, keys, values, betas, gate, norm_gain):
    beta_rows = betas.astype(f32).transpose(2, 0, 1).reshape(H, 1, STEPS)
    here = pl.BlockSpec(memory_space=pltpu.VMEM)
    vm = pltpu.VMEM
    dma = pltpu.SemaphoreType.DMA
    tile = (DK, DK)
    return pl.pallas_call(
        layer_kernel,
        in_specs=[here] * 6,
        out_specs=here,
        out_shape=jax.ShapeDtypeStruct((CT, H * DK), bf16),
        scratch_shapes=[
            vm((LEVELS, STEPS, STEPS), bf16),
            vm((H, CT, DK), f32),
            vm((H, CT, DK), f32),
            vm((3, 8, 4) + tile, bf16),
            vm((8, 3) + tile, bf16),
            vm((4, 2, 3) + tile, bf16),
            vm((2, 4, 2) + tile, bf16),
            vm((2, 4) + tile, f32),
            vm((4, 2, 3) + tile, bf16),
            vm((2, 4, 2) + tile, bf16),
            vm((2, 4) + tile, f32),
            vm((2, 2) + tile, bf16),
            vm((2,) + tile, f32),
            vm((2,) + tile, bf16),
            vm((2,) + tile, bf16),
            vm((4, 2) + tile, bf16),
            vm((8,) + tile, bf16),
            vm((8,) + tile, bf16),
            vm((8,) + tile, bf16),
            vm((8,) + tile, bf16),
            dma((8,)),
            dma((8,)),
            dma((4, 2)),
            dma((4, 2)),
            dma((4, 2)),
            dma((4, 2)),
            dma((2,)),
            dma((2,)),
            dma((4, 2)),
            dma((8,)),
            dma((8,)),
            dma((8,)),
            dma((2,)),
        ],
        compiler_params=pltpu.CompilerParams(
            collective_id=0, has_side_effects=True, vmem_limit_bytes=60 << 20
        ),
    )(queries, keys, values, beta_rows, gate, norm_gain.reshape(1, DK))


def solution(mesh):
    torus = Mesh(mesh.devices.reshape(4, 4, 4, 2), AXES)
    rows, pairs = P(AXES, None), P(AXES, None, None)
    return jax.shard_map(
        shards, mesh=torus, in_specs=(rows, pairs, pairs, pairs, rows, P()), out_specs=rows, check_vma=False
    )
```

```python
import functools

import jax
import jax.numpy as jnp
from jax import lax
from jax.experimental import pallas as pl
from jax.experimental.pallas import tpu as pltpu
from jax.sharding import Mesh
from jax.sharding import PartitionSpec as P

H = 16
DK = 256
CT = 128
STEPS = 256
EPS = 1e-06
LEVELS = 8
HALF = 128
f32 = jnp.float32
bf16 = jnp.bfloat16
AXES = ("z", "y", "x", "core")
MESH = pl.DeviceIdType.MESH


def mm(a, b, dims=((1,), (0,))):
    return lax.dot_general(a, b, (dims, ((), ())), preferred_element_type=f32)


def split(x):
    hi = x.astype(bf16)
    return hi, (x - hi.astype(f32)).astype(bf16)


def mm_right(a, b):
    hi, lo = b
    return mm(a, hi) + mm(a, lo)


def mm_both(a, b):
    return mm(a[0], b[0]) + (mm(a[0], b[1]) + mm(a[1], b[0]))


def factors(ks, vs, beta_rows, mask_ref):
    row = lax.broadcasted_iota(jnp.int32, (STEPS, STEPS), 0)
    col = lax.broadcasted_iota(jnp.int32, (STEPS, STEPS), 1)
    eye = row == col
    eye_h = eye[:HALF, :HALF]
    n = range(len(ks))
    both = range(2)
    part = (slice(0, HALF), slice(HALF, STEPS))
    gram = [mm(k, k, ((1,), (1,))) for k in ks]
    g = [jnp.sum(jnp.where(eye, x, 0.0), axis=0, keepdims=True) + EPS for x in gram]
    c = [beta_rows[i] / g[i] for i in n]
    low = [split(jnp.where(row > col, x, 0.0)) for x in gram]
    tau = [[jnp.where(eye_h, c[i][:, part[j]], 0.0) for j in both] for i in n]
    diag = [[low[i][0][part[j], part[j]] for j in both] for i in n]
    for level in range(LEVELS - 1):
        edge = [[x * mask_ref[level] for x in d] for d in diag]
        tb = [[x.astype(bf16) for x in t] for t in tau]
        if level == 0:
            step = [
                [(edge[i][j].astype(f32) * c[i][:, part[j]]).astype(bf16) for j in both] for i in n
            ]
        else:
            step = [[mm(edge[i][j], tb[i][j]).astype(bf16) for j in both] for i in n]
        tau = [[tau[i][j] - mm(tb[i][j], step[i][j]) for j in both] for i in n]
    tb = [[x.astype(bf16) for x in t] for t in tau]
    step = [mm(low[i][0][part[1], part[0]], tb[i][0]).astype(bf16) for i in n]
    below = [-mm(tb[i][1], step[i]) for i in n]
    zero = jnp.zeros((HALF, HALF), bf16)
    tb = [
        jnp.concatenate(
            [
                jnp.concatenate([tb[i][0], zero], axis=1),
                jnp.concatenate([below[i].astype(bf16), tb[i][1]], axis=1),
            ],
            axis=0,
        )
        for i in n
    ]
    t32 = [x.astype(f32) for x in tb]
    rest = [
        jnp.where(eye, 1.0, 0.0) - t32[i] * (g[i] / beta_rows[i]) - mm_right(tb[i], low[i]) for i in n
    ]
    tau = [t32[i] + mm(rest[i].astype(bf16), tb[i]) for i in n]
    ts = [split(x) for x in tau]
    w = [split(mm(ts[i][0], ks[i]) + mm(ts[i][1], ks[i])) for i in n]
    ts = [split(tau[i] * jnp.sqrt(g[i])) for i in n]
    y = [split(mm(ts[i][0], vs[i]) + mm(ts[i][1], vs[i])) for i in n]
    kt = [k.T for k in ks]
    a = [jnp.where(eye, 1.0, 0.0) - mm_right(kt[i], w[i]) for i in n]
    b = [mm_right(kt[i], y[i]) for i in n]
    return a, b, w, y


def answers(ks, qs, w, y):
    n = range(len(ks))
    token = lax.broadcasted_iota(jnp.int32, (CT, STEPS), 0)
    step_of = lax.broadcasted_iota(jnp.int32, (CT, STEPS), 1)
    causal = step_of // 2 <= token
    p = [split(jnp.where(causal, mm(qs[i], ks[i], ((1,), (1,))), 0.0)) for i in n]
    q32 = [q.astype(f32) for q in qs]
    unit = [lax.rsqrt(jnp.sum(q * q, axis=-1, keepdims=True) + EPS) for q in q32]
    qt = [(q32[i] - mm_both(p[i], w[i])) * unit[i] for i in n]
    ot = [mm_both(p[i], y[i]) * unit[i] for i in n]
    return qt, ot


def make_masks(mask_ref):
    row = lax.broadcasted_iota(jnp.int32, (HALF, HALF), 0)
    col = lax.broadcasted_iota(jnp.int32, (HALF, HALF), 1)
    differ = jnp.bitwise_xor(row, col)
    for level in range(LEVELS - 1):
        inside = (differ >= (1 << level)) & (differ < (2 << level))
        mask_ref[level] = jnp.where(inside, 1.0, 0.0).astype(bf16)


def gated(o, gain, gate):
    scale = lax.rsqrt(jnp.mean(o * o, axis=-1, keepdims=True) + EPS)
    normed = (o * scale * gain).astype(bf16).astype(f32)
    gate = gate.astype(f32)
    return (normed * (gate / (1.0 + jnp.exp(-gate)))).astype(bf16)


def put_pair(ref, values):
    ref[0], ref[1] = split(values)


def layer_kernel(
    q_ref, k_ref, v_ref, beta_ref, gate_ref, gain_ref, out_ref,
    mask, wy, blk, x_out, x_in, pxa, pxb, y_out, y_in, pya, pyb, z_in, z_out, u_out, u_in,
    s_out, s_in, mine, c_out, c_in,
    core_send, core_recv, x_send, x_recv, y_send, y_recv, z_send, z_recv, u_send, u_recv, s_send, s_recv,
    c_send, c_recv, here,
):
    z, y, x, c = (lax.axis_index(name) for name in AXES)
    other = {"core": 1 - c}

    def along(axis, index, offset):
        return {axis: lax.rem(index + offset, 4)}

    barrier = pltpu.get_barrier_semaphore()
    greeted = [other] + [along("x", x, o) for o in (1, 2, 3)] + [along("y", y, o) for o in (1, 2, 3)]
    greeted += [along("z", z, o) for o in (1, 3)]
    for device in greeted:
        pl.semaphore_signal(barrier, inc=1, device_id=device, device_id_type=MESH)

    def remote(src, dst, send, recv, device):
        return pltpu.make_async_remote_copy(
            src_ref=src, dst_ref=dst, send_sem=send, recv_sem=recv, device_id=device, device_id_type=MESH
        )

    def core_copy(j, slot):
        return remote(blk.at[2, j], blk.at[slot, j], core_send.at[j], core_recv.at[j], other)

    def x_copy(i, o, j, source):
        return remote(
            x_out.at[j], x_in.at[source, i], x_send.at[o, i], x_recv.at[source, i], along("x", x, o)
        )

    def y_copy(i, source, root):
        return remote(y_out.at[i], y_in.at[source], y_send.at[i], y_recv.at[source], {"y": root})

    def z_copy():
        return remote(z_out, z_in, z_send.at[0], z_recv.at[0], along("z", z, 1))

    def u_copy(i, o, dest):
        return remote(u_out.at[dest], u_in.at[i], u_send.at[o], u_recv.at[i], {"y": dest})

    def s_copy(i, o, dest, source):
        j = 2 * source + i
        return remote(s_out.at[dest, i], s_in.at[j], s_send.at[o, i], s_recv.at[j], along("x", x, o))

    def c_copy(j):
        return remote(c_out.at[j], c_in.at[j], c_send.at[j], c_recv.at[j], other)

    def lanes_of(head):
        return pl.ds(pl.multiple_of(head * DK, DK), DK)

    make_masks(mask)

    def phase(p, carry):
        i, own = p // 2, p % 2
        group = own * c + (1 - own) * (1 - c)
        slot = own * c + (1 - own) * 2
        heads = [8 * group + 2 * n + i for n in range(4)]
        lanes = [lanes_of(h) for h in heads]
        a, b, w, y = factors(
            [k_ref[:, :, n].reshape(STEPS, DK) for n in lanes],
            [v_ref[:, :, n].reshape(STEPS, DK) for n in lanes],
            [beta_ref[h] for h in heads],
            mask,
        )
        for n in range(4):
            j = 2 * n + i
            put_pair(blk.at[slot, j, pl.ds(0, 2)], a[n])
            put_pair(blk.at[slot, j, pl.ds(2, 2)], b[n])
            wy[heads[n], 0], wy[heads[n], 1] = w[n]
            wy[heads[n], 2], wy[heads[n], 3] = y[n]

        @pl.when(p == 0)
        def _():
            pl.semaphore_wait(barrier, len(greeted))

        @pl.when(own == 0)
        def _():
            for n in range(4):
                core_copy(2 * n + i, c).start()

        @pl.when(own == 1)
        def _():
            for o in (1, 3, 2, 0):
                dest = lax.rem(x + o, 4)
                j = 2 * dest + i
                core_copy(j, 1 - c).wait_recv()
                later = (blk[1, j, 0], blk[1, j, 1])
                put_pair(x_out.at[j, pl.ds(0, 2)], mm_both(later, (blk[0, j, 0], blk[0, j, 1])))
                x_out[j, 2] = (
                    mm_both(later, (blk[0, j, 2], blk[0, j, 3]))
                    + blk[1, j, 2].astype(f32)
                    + blk[1, j, 3].astype(f32)
                ).astype(bf16)
                if o:
                    x_copy(i, o, j, x).start()
                else:
                    pltpu.make_async_copy(x_out.at[j], x_in.at[x, i], here.at[i]).start()

        return carry

    lax.fori_loop(0, 4, phase, 0)

    def answer(p, carry):
        heads = [4 * p + n for n in range(4)]
        lanes = [lanes_of(h) for h in heads]
        q_now, o_now = answers(
            [k_ref[:, :, n].reshape(STEPS, DK) for n in lanes],
            [q_ref[:, n] for n in lanes],
            [(wy[h, 0], wy[h, 1]) for h in heads],
            [(wy[h, 2], wy[h, 3]) for h in heads],
        )
        for n in range(4):
            h = heads[n]
            wy[h, 0, :CT], wy[h, 0, CT:] = split(q_now[n])
            wy[h, 1, :CT], wy[h, 1, CT:] = split(o_now[n])
        return carry

    lax.fori_loop(0, 4, answer, 0)

    def compose(pairs, pa, pb):
        eye = lax.broadcasted_iota(jnp.int32, (DK, DK), 0) == lax.broadcasted_iota(jnp.int32, (DK, DK), 1)
        pa[0, 0] = jnp.where(eye, 1.0, 0.0).astype(bf16)
        pa[0, 1] = jnp.zeros((DK, DK), bf16)
        pb[0] = jnp.zeros((DK, DK), f32)
        a = (pairs[0, 0], pairs[0, 1])
        b = pairs[0, 2].astype(f32)
        for n in range(1, 4):
            pa[n, 0], pa[n, 1] = a
            pb[n] = b
            later = (pairs[n, 0], pairs[n, 1])
            a = split(mm_both(later, a))
            b = mm_both(later, split(b)) + pairs[n, 2].astype(f32)
        return a, b

    def over_x(i):
        pltpu.make_async_copy(x_out.at[2 * x + i], x_in.at[x, i], here.at[i]).wait()
        for o in (1, 3, 2):
            source = lax.rem(x + o, 4)
            x_copy(i, o, 2 * source + i, source).wait_recv()
        a, b = compose(x_in.at[:, i], pxa.at[i], pxb.at[i])
        root = 2 * c + i

        @pl.when(y == root)
        def _():
            y_in[y, 0], y_in[y, 1] = a
            y_in[y, 2] = b.astype(bf16)

        @pl.when(y != root)
        def _():
            y_out[i, 0], y_out[i, 1] = a
            y_out[i, 2] = b.astype(bf16)
            y_copy(i, y, root).start()

    i_root = y % 2
    is_root = y // 2 == c

    def over_y():
        for o in (1, 3, 2):
            y_copy(i_root, lax.rem(y + o, 4), y).wait_recv()
        a, b = compose(y_in, pya, pyb)
        z_out[...] = b.astype(bf16)
        pya[4, 0], pya[4, 1] = a
        pyb[4] = b

    def over_z():
        @pl.when(z == 0)
        def _():
            z_in[...] = jnp.zeros((DK, DK), bf16)

        @pl.when(z > 0)
        def _():
            z_copy().wait_recv()
            z_out[...] = (mm(pya[4, 0], z_in[...]) + mm(pya[4, 1], z_in[...]) + pyb[4]).astype(bf16)

        @pl.when(z < 3)
        def _():
            z_copy().start()

        for o in (1, 3, 2, 0):
            dest = lax.rem(y + o, 4)
            now = mm(pya[dest, 0], z_in[...]) + mm(pya[dest, 1], z_in[...]) + pyb[dest]
            if o:
                put_pair(u_out.at[dest], now)
                u_copy(i_root, o, dest).start()
            else:
                put_pair(u_in.at[i_root], now)

    def down(i):
        root = 2 * c + i

        @pl.when(y != root)
        def _():
            u_copy(i, 1, y).wait_recv()

        s = (u_in[i, 0], u_in[i, 1])
        for o in (1, 3, 2, 0):
            dest = lax.rem(x + o, 4)
            now = (mm_both((pxa[i, dest, 0], pxa[i, dest, 1]), s) + pxb[i, dest]).astype(bf16)
            if o:
                s_out[dest, i] = now
                s_copy(i, o, dest, x).start()
            else:
                s_in[2 * x + i] = now

    first_root = is_root & (i_root == 0)
    second_root = is_root & (i_root == 1)
    over_x(0)
    pl.when(first_root)(over_y)
    over_x(1)
    pl.when(first_root)(over_z)
    pl.when(second_root)(over_y)
    pl.when(second_root & (z < 2))(over_z)
    down(0)
    pl.when(second_root & (z >= 2))(over_z)
    down(1)

    def over_cores(i, carry):
        for o in (0, 1, 3, 2):
            source = lax.rem(x + o, 4)
            j = 2 * source + i
            if o:
                s_copy(i, o, source, source).wait_recv()
            first = s_in[j]
            second = (
                mm(blk[0, j, 0], first)
                + mm(blk[0, j, 1], first)
                + blk[0, j, 2].astype(f32)
                + blk[0, j, 3].astype(f32)
            ).astype(bf16)
            mine[j] = jnp.where(c == 0, first, second)
            c_out[j] = jnp.where(c == 0, second, first)
            c_copy(j).start()
        return carry

    lax.fori_loop(0, 2, over_cores, 0)

    def finish(head, state):
        o = mm(wy[head, 0, :CT], state) + mm(wy[head, 0, CT:], state)
        o += wy[head, 1, :CT].astype(f32) + wy[head, 1, CT:].astype(f32)
        lanes = lanes_of(head)
        out_ref[:, lanes] = gated(o, gain_ref[...], gate_ref[:, lanes])

    def last_own(j, carry):
        finish(8 * c + j, mine[j])
        return carry

    def last_other(j, carry):
        c_copy(j).wait_recv()
        finish(8 * (1 - c) + j, c_in[j])
        return carry

    lax.fori_loop(0, 8, last_own, 0)
    lax.fori_loop(0, 8, last_other, 0)

    def drain(j, carry):
        core_copy(j, c).wait_send()
        c_copy(j).wait_send()
        return carry

    def drain_links(i, carry):
        for o in (1, 2, 3):
            dest = lax.rem(x + o, 4)
            x_copy(i, o, 2 * dest + i, x).wait_send()
            s_copy(i, o, dest, x).wait_send()

        @pl.when(y != 2 * c + i)
        def _():
            y_copy(i, y, 2 * c + i).wait_send()

        return carry

    lax.fori_loop(0, 8, drain, 0)
    lax.fori_loop(0, 2, drain_links, 0)

    @pl.when(is_root)
    def _():
        for o in (1, 2, 3):
            u_copy(i_root, o, lax.rem(y + o, 4)).wait_send()

        @pl.when(z < 3)
        def _():
            z_copy().wait_send()


def shards(queries, keys, values, betas, gate, norm_gain):
    beta_rows = betas.astype(f32).transpose(2, 0, 1).reshape(H, 1, STEPS)
    here = pl.BlockSpec(memory_space=pltpu.VMEM)
    vm = pltpu.VMEM
    dma = pltpu.SemaphoreType.DMA
    tile = (DK, DK)
    return pl.pallas_call(
        layer_kernel,
        in_specs=[here] * 6,
        out_specs=here,
        out_shape=jax.ShapeDtypeStruct((CT, H * DK), bf16),
        scratch_shapes=[
            vm((LEVELS - 1, HALF, HALF), bf16),
            vm((H, 4) + tile, bf16),
            vm((3, 8, 4) + tile, bf16),
            vm((8, 3) + tile, bf16),
            vm((4, 2, 3) + tile, bf16),
            vm((2, 4, 2) + tile, bf16),
            vm((2, 4) + tile, f32),
            vm((2, 3) + tile, bf16),
            vm((4, 3) + tile, bf16),
            vm((5, 2) + tile, bf16),
            vm((5,) + tile, f32),
            vm(tile, bf16),
            vm(tile, bf16),
            vm((4, 2) + tile, bf16),
            vm((2, 2) + tile, bf16),
            vm((4, 2) + tile, bf16),
            vm((8,) + tile, bf16),
            vm((8,) + tile, bf16),
            vm((8,) + tile, bf16),
            vm((8,) + tile, bf16),
            dma((8,)),
            dma((8,)),
            dma((4, 2)),
            dma((4, 2)),
            dma((2,)),
            dma((4,)),
            dma((1,)),
            dma((1,)),
            dma((4,)),
            dma((2,)),
            dma((4, 2)),
            dma((8,)),
            dma((8,)),
            dma((8,)),
            dma((2,)),
        ],
        compiler_params=pltpu.CompilerParams(
            collective_id=0, has_side_effects=True, vmem_limit_bytes=60 << 20
        ),
    )(queries, keys, values, beta_rows, gate, norm_gain.reshape(1, DK))


def solution(mesh):
    torus = Mesh(mesh.devices.reshape(4, 4, 4, 2), AXES)
    rows, pairs = P(AXES, None), P(AXES, None, None)
    return jax.shard_map(
        shards, mesh=torus, in_specs=(rows, pairs, pairs, pairs, rows, P()), out_specs=rows, check_vma=False
    )
```

```python
import functools

import jax
import jax.numpy as jnp
from jax import lax
from jax.experimental import pallas as pl
from jax.experimental.pallas import tpu as pltpu
from jax.sharding import Mesh
from jax.sharding import PartitionSpec as P

H = 16
DK = 256
CT = 128
STEPS = 256
EPS = 1e-06
LEVELS = 8
HALF = 128
f32 = jnp.float32
bf16 = jnp.bfloat16
AXES = ("z", "y", "x", "core")
MESH = pl.DeviceIdType.MESH


def mm(a, b, dims=((1,), (0,))):
    return lax.dot_general(a, b, (dims, ((), ())), preferred_element_type=f32)


def split(x):
    hi = x.astype(bf16)
    return hi, (x - hi.astype(f32)).astype(bf16)


def mm_right(a, b):
    hi, lo = b
    return mm(a, hi) + mm(a, lo)


def mm_both(a, b):
    return mm(a[0], b[0]) + (mm(a[0], b[1]) + mm(a[1], b[0]))


def factors(ks, vs, beta_rows, mask_ref):
    row = lax.broadcasted_iota(jnp.int32, (STEPS, STEPS), 0)
    col = lax.broadcasted_iota(jnp.int32, (STEPS, STEPS), 1)
    eye = row == col
    eye_h = eye[:HALF, :HALF]
    n = range(len(ks))
    both = range(2)
    part = (slice(0, HALF), slice(HALF, STEPS))
    gram = [mm(k, k, ((1,), (1,))) for k in ks]
    g = [jnp.sum(jnp.where(eye, x, 0.0), axis=0, keepdims=True) + EPS for x in gram]
    c = [beta_rows[i] / g[i] for i in n]
    low = [split(jnp.where(row > col, x, 0.0)) for x in gram]
    tau = [[jnp.where(eye_h, c[i][:, part[j]], 0.0) for j in both] for i in n]
    diag = [[low[i][0][part[j], part[j]] for j in both] for i in n]
    for level in range(LEVELS - 1):
        edge = [[x * mask_ref[level] for x in d] for d in diag]
        tb = [[x.astype(bf16) for x in t] for t in tau]
        if level == 0:
            step = [
                [(edge[i][j].astype(f32) * c[i][:, part[j]]).astype(bf16) for j in both] for i in n
            ]
        else:
            step = [[mm(edge[i][j], tb[i][j]).astype(bf16) for j in both] for i in n]
        tau = [[tau[i][j] - mm(tb[i][j], step[i][j]) for j in both] for i in n]
    tb = [[x.astype(bf16) for x in t] for t in tau]
    step = [mm(low[i][0][part[1], part[0]], tb[i][0]).astype(bf16) for i in n]
    below = [-mm(tb[i][1], step[i]) for i in n]
    zero = jnp.zeros((HALF, HALF), bf16)
    tb = [
        jnp.concatenate(
            [
                jnp.concatenate([tb[i][0], zero], axis=1),
                jnp.concatenate([below[i].astype(bf16), tb[i][1]], axis=1),
            ],
            axis=0,
        )
        for i in n
    ]
    t32 = [x.astype(f32) for x in tb]
    rest = [
        jnp.where(eye, 1.0, 0.0) - t32[i] * (g[i] / beta_rows[i]) - mm_right(tb[i], low[i]) for i in n
    ]
    tau = [t32[i] + mm(rest[i].astype(bf16), tb[i]) for i in n]
    ts = [split(x) for x in tau]
    w = [split(mm(ts[i][0], ks[i]) + mm(ts[i][1], ks[i])) for i in n]
    ts = [split(tau[i] * jnp.sqrt(g[i])) for i in n]
    y = [split(mm(ts[i][0], vs[i]) + mm(ts[i][1], vs[i])) for i in n]
    kt = [k.T for k in ks]
    a = [jnp.where(eye, 1.0, 0.0) - mm_right(kt[i], w[i]) for i in n]
    b = [mm_right(kt[i], y[i]) for i in n]
    return a, b, w, y


def answers(ks, qs, w, y):
    n = range(len(ks))
    token = lax.broadcasted_iota(jnp.int32, (CT, STEPS), 0)
    step_of = lax.broadcasted_iota(jnp.int32, (CT, STEPS), 1)
    causal = step_of // 2 <= token
    p = [split(jnp.where(causal, mm(qs[i], ks[i], ((1,), (1,))), 0.0)) for i in n]
    q32 = [q.astype(f32) for q in qs]
    unit = [lax.rsqrt(jnp.sum(q * q, axis=-1, keepdims=True) + EPS) for q in q32]
    qt = [(q32[i] - mm_both(p[i], w[i])) * unit[i] for i in n]
    ot = [mm_both(p[i], y[i]) * unit[i] for i in n]
    return qt, ot


def make_masks(mask_ref):
    row = lax.broadcasted_iota(jnp.int32, (HALF, HALF), 0)
    col = lax.broadcasted_iota(jnp.int32, (HALF, HALF), 1)
    differ = jnp.bitwise_xor(row, col)
    for level in range(LEVELS - 1):
        inside = (differ >= (1 << level)) & (differ < (2 << level))
        mask_ref[level] = jnp.where(inside, 1.0, 0.0).astype(bf16)


def put_pair(ref, values):
    ref[0], ref[1] = split(values)


def layer_kernel(
    q_hbm, k_hbm, v_hbm, beta_ref, gain_ref, out_ref,
    q_ref, k_ref, v_ref, beta, mask, wy, blk, x_out, x_in, pxa, pxb, y_out, y_in, pf_out, pf_in, line, line_in,
    z_in, z_mid, z_out, u_in,
    s_out, s_in, mine, c_out, c_in,
    core_send, core_recv, x_send, x_recv, y_send, y_recv, z_send, z_recv, p_send, p_recv, u_send, u_recv, s_send, s_recv,
    c_send, c_recv, q_here, k_here, v_here,
):
    z, y, x, c = (lax.axis_index(name) for name in AXES)
    other = {"core": 1 - c}

    def along(axis, index, offset):
        return {axis: lax.rem(index + offset, 4)}

    barrier = pltpu.get_barrier_semaphore()
    greeted = [other] + [along("x", x, o) for o in (1, 2, 3)] + [along("y", y, o) for o in (1, 2, 3)]
    greeted += [along("z", z, o) for o in (1, 2, 3)]
    for device in greeted:
        pl.semaphore_signal(barrier, inc=1, device_id=device, device_id_type=MESH)

    def remote(src, dst, send, recv, device):
        return pltpu.make_async_remote_copy(
            src_ref=src, dst_ref=dst, send_sem=send, recv_sem=recv, device_id=device, device_id_type=MESH
        )

    def core_copy(j, slot):
        return remote(blk.at[2, j], blk.at[slot, j], core_send.at[j], core_recv.at[j], other)

    def x_copy(i, o, j, source):
        return remote(
            x_out.at[j], x_in.at[source, i], x_send.at[o, i], x_recv.at[source, i], along("x", x, o)
        )

    def y_copy(i, source, root):
        return remote(y_out.at[i], y_in.at[source], y_send.at[i], y_recv.at[source], {"y": root})

    def z_next(source):
        return remote(source, z_in, z_send.at[0], z_recv.at[0], along("z", z, 1))

    def z_skip():
        return remote(z_out, z_mid, z_send.at[1], z_recv.at[1], along("z", z, 2))

    def line_copy():
        return remote(line, line_in, z_send.at[2], z_recv.at[2], along("z", z, 1))

    def p_copy(i, o, dest):
        return remote(pf_out.at[dest], pf_in.at[i], p_send.at[o], p_recv.at[i], {"y": dest})

    def u_copy(i, o, dest):
        return remote(z_in, u_in.at[i], u_send.at[o], u_recv.at[i], {"y": dest})

    def s_copy(i, o, dest, source):
        j = 2 * source + i
        return remote(s_out.at[dest, i], s_in.at[j], s_send.at[o, i], s_recv.at[j], along("x", x, o))

    def c_copy(j):
        return remote(c_out.at[j], c_in.at[j], c_send.at[j], c_recv.at[j], other)

    def lanes_of(head):
        return pl.ds(pl.multiple_of(head * DK, DK), DK)

    def load(head):
        lanes = lanes_of(head)
        return (
            pltpu.make_async_copy(k_hbm.at[:, :, lanes], k_ref.at[:, :, lanes], k_here.at[head]),
            pltpu.make_async_copy(v_hbm.at[:, :, lanes], v_ref.at[:, :, lanes], v_here.at[head]),
        )

    def place(own, j):
        return own * c + (1 - own) * 2, 8 * (own * c + (1 - own) * (1 - c)) + j

    def away(p):
        own = p % 2
        return [(own, 2 * lax.rem(x + o, 4) + p // 2) for o in (1, 3, 2)]

    near = [(own, 2 * x + i) for own in (0, 1) for i in (0, 1)]

    def start_loads(group):
        for own, j in group:
            for copy in load(place(own, j)[1]):
                copy.start()

    def loads_of(p, carry):
        start_loads(away(p))
        return carry

    lax.fori_loop(0, 4, loads_of, 0)
    start_loads(near)
    q_load = pltpu.make_async_copy(q_hbm, q_ref, q_here.at[0])
    q_load.start()

    make_masks(mask)
    token = lax.broadcasted_iota(jnp.int32, (CT, STEPS), 0)
    step_of = lax.broadcasted_iota(jnp.int32, (CT, STEPS), 1)
    spread = [jnp.where(step_of == 2 * token + r, 1.0, 0.0).astype(bf16) for r in (0, 1)]
    beta[...] = mm(beta_ref[0], spread[0]) + mm(beta_ref[1], spread[1])

    def make_pairs(group):
        places = [place(own, j) for own, j in group]
        for slot, head in places:
            for copy in load(head):
                copy.wait()
        lanes = [lanes_of(head) for slot, head in places]
        a, b, w, y_rows = factors(
            [k_ref[:, :, n].reshape(STEPS, DK) for n in lanes],
            [v_ref[:, :, n].reshape(STEPS, DK) for n in lanes],
            [beta[pl.ds(head, 1), :] for slot, head in places],
            mask,
        )
        for n, (slot, head) in enumerate(places):
            j = group[n][1]
            put_pair(blk.at[slot, j, pl.ds(0, 2)], a[n])
            put_pair(blk.at[slot, j, pl.ds(2, 2)], b[n])
            wy[head, 0], wy[head, 1] = w[n]
            wy[head, 2], wy[head, 3] = y_rows[n]

    def merge(j, pair):
        core_copy(j, 1 - c).wait_recv()
        later = (blk[1, j, 0], blk[1, j, 1])
        put_pair(pair.at[pl.ds(0, 2)], mm_both(later, (blk[0, j, 0], blk[0, j, 1])))
        pair[2] = (
            mm_both(later, (blk[0, j, 2], blk[0, j, 3]))
            + blk[1, j, 2].astype(f32)
            + blk[1, j, 3].astype(f32)
        ).astype(bf16)

    def phase(p, carry):
        i = p // 2
        group = away(p)
        make_pairs(group)

        @pl.when(p == 0)
        def _():
            pl.semaphore_wait(barrier, len(greeted))

        @pl.when(p % 2 == 0)
        def _():
            for own, j in group:
                core_copy(j, c).start()

        @pl.when(p % 2 == 1)
        def _():
            for o in (1, 3, 2):
                j = 2 * lax.rem(x + o, 4) + i
                merge(j, x_out.at[j])
                x_copy(i, o, j, x).start()

        return carry

    lax.fori_loop(0, 4, phase, 0)
    make_pairs(near)
    for i in (0, 1):
        core_copy(2 * x + i, c).start()
    q_load.wait()

    def answer(p, carry):
        heads = [4 * p + n for n in range(4)]
        lanes = [lanes_of(h) for h in heads]
        q_now, o_now = answers(
            [k_ref[:, :, n].reshape(STEPS, DK) for n in lanes],
            [q_ref[:, n] for n in lanes],
            [(wy[h, 0], wy[h, 1]) for h in heads],
            [(wy[h, 2], wy[h, 3]) for h in heads],
        )
        for n in range(4):
            h = heads[n]
            wy[h, 0, :CT], wy[h, 0, CT:] = split(q_now[n])
            wy[h, 1, :CT], wy[h, 1, CT:] = split(o_now[n])
        return carry

    lax.fori_loop(0, 4, answer, 0)
    for i in (0, 1):
        merge(2 * x + i, x_in.at[x, i])

    def compose(pairs, whole, prefix):
        p = [(pairs[n, 0], pairs[n, 1]) for n in range(4)]
        b = [pairs[n, 2] for n in range(4)]
        a10, a32 = split(mm_both(p[1], p[0])), split(mm_both(p[3], p[2]))
        b10 = mm(p[1][0], b[0]) + mm(p[1][1], b[0]) + b[1].astype(f32)
        b32 = mm(p[3][0], b[2]) + mm(p[3][1], b[2]) + b[3].astype(f32)
        b10s = split(b10)
        whole(split(mm_both(a32, a10)), mm_both(a32, b10s) + b32)
        prefix(1, p[0], b[0].astype(f32))
        prefix(2, a10, b10)
        prefix(3, split(mm_both(p[2], a10)), mm_both(p[2], b10s) + b[2].astype(f32))

    def identity():
        eye = lax.broadcasted_iota(jnp.int32, (DK, DK), 0) == lax.broadcasted_iota(jnp.int32, (DK, DK), 1)
        return jnp.where(eye, 1.0, 0.0).astype(bf16), jnp.zeros((DK, DK), bf16)

    for i in (0, 1):
        pxa[i, 0, 0], pxa[i, 0, 1] = identity()
        pxb[i, 0] = jnp.zeros((DK, DK), f32)

    def over_x(i):
        for o in (1, 3, 2):
            source = lax.rem(x + o, 4)
            x_copy(i, o, 2 * source + i, source).wait_recv()
        root = 2 * c + i

        def whole(a, b):
            @pl.when(y == root)
            def _():
                y_in[y, 0], y_in[y, 1] = a
                y_in[y, 2] = b.astype(bf16)

            @pl.when(y != root)
            def _():
                y_out[i, 0], y_out[i, 1] = a
                y_out[i, 2] = b.astype(bf16)
                y_copy(i, y, root).start()

        def prefix(n, a, b):
            pxa[i, n, 0], pxa[i, n, 1] = a
            pxb[i, n] = b

        compose(x_in.at[:, i], whole, prefix)

    i_root = y % 2
    is_root = y // 2 == c

    def over_y():
        for o in (1, 3, 2):
            y_copy(i_root, lax.rem(y + o, 4), y).wait_recv()

        def whole(a, b):
            line[0], line[1] = a
            line[2], line[3] = split(b)

            @pl.when(z == 0)
            def _():
                z_next(line.at[2]).start()

            @pl.when(z == 2)
            def _():
                line_copy().start()

        def prefix(n, a, b):
            pf_out[n, 0], pf_out[n, 1] = a
            pf_out[n, 2], pf_out[n, 3] = split(b)

        compose(y_in, whole, prefix)
        for o in (1, 2, 3):
            dest = lax.rem(y + o, 4)

            @pl.when(dest > 0)
            def _():
                p_copy(i_root, o, dest).start()

        @pl.when(y > 0)
        def _():
            for n in range(4):
                pf_in[i_root, n] = pf_out[y, n]

    def advance(pair, s):
        out = mm(pair[0], s) + mm(pair[1], s)
        return out + pair[2].astype(f32) + pair[3].astype(f32)

    def over_z():
        @pl.when(z == 0)
        def _():
            z_in[...] = jnp.zeros((DK, DK), bf16)

        @pl.when(z == 1)
        def _():
            z_next(z_out).wait_recv()
            z_out[...] = advance(line, z_in[...]).astype(bf16)
            z_skip().start()
            z_next(z_out).start()

        @pl.when(z == 2)
        def _():
            z_next(z_out).wait_recv()

        @pl.when(z == 3)
        def _():
            line_copy().wait_recv()
            z_skip().wait_recv()
            z_in[...] = advance(line_in, z_mid[...]).astype(bf16)

        for o in (2, 1, 3):
            u_copy(i_root, o, lax.rem(y + o, 4)).start()
        u_in[i_root] = z_in[...]

    def down(i):
        root = 2 * c + i

        @pl.when(y == 0)
        def _():
            pf_in[i, 0], pf_in[i, 1] = identity()
            pf_in[i, 2] = jnp.zeros((DK, DK), bf16)
            pf_in[i, 3] = jnp.zeros((DK, DK), bf16)

        @pl.when((y != root) & (y > 0))
        def _():
            p_copy(i, 1, y).wait_recv()

        @pl.when(y != root)
        def _():
            u_copy(i, 1, y).wait_recv()

        s = split(advance(pf_in.at[i], u_in[i]))
        for o in (1, 3, 2, 0):
            dest = lax.rem(x + o, 4)
            now = (mm_both((pxa[i, dest, 0], pxa[i, dest, 1]), s) + pxb[i, dest]).astype(bf16)
            if o:
                s_out[dest, i] = now
                s_copy(i, o, dest, x).start()
            else:
                s_in[2 * x + i] = now

    first_root = is_root & (i_root == 0)
    second_root = is_root & (i_root == 1)
    over_x(0)
    pl.when(first_root)(over_y)
    over_x(1)
    pl.when(first_root)(over_z)
    pl.when(second_root)(over_y)
    pl.when(second_root & (z < 2))(over_z)
    down(0)
    pl.when(second_root & (z >= 2))(over_z)
    down(1)

    def over_cores(i, carry):
        for o in (0, 1, 3, 2):
            source = lax.rem(x + o, 4)
            j = 2 * source + i
            if o:
                s_copy(i, o, source, source).wait_recv()
            first = s_in[j]
            second = (
                mm(blk[0, j, 0], first)
                + mm(blk[0, j, 1], first)
                + blk[0, j, 2].astype(f32)
                + blk[0, j, 3].astype(f32)
            ).astype(bf16)
            mine[j] = jnp.where(c == 0, first, second)
            c_out[j] = jnp.where(c == 0, second, first)
            c_copy(j).start()
        return carry

    lax.fori_loop(0, 2, over_cores, 0)

    def finish(head, state):
        o = mm(wy[head, 0, :CT], state) + mm(wy[head, 0, CT:], state)
        o += wy[head, 1, :CT].astype(f32) + wy[head, 1, CT:].astype(f32)
        scale = lax.rsqrt(jnp.mean(o * o, axis=-1, keepdims=True) + EPS)
        out_ref[:, lanes_of(head)] = (o * scale * gain_ref[...]).astype(bf16)

    def last_own(j, carry):
        finish(8 * c + j, mine[j])
        return carry

    def last_other(j, carry):
        c_copy(j).wait_recv()
        finish(8 * (1 - c) + j, c_in[j])
        return carry

    lax.fori_loop(0, 8, last_own, 0)
    lax.fori_loop(0, 8, last_other, 0)

    def drain(j, carry):
        core_copy(j, c).wait_send()
        c_copy(j).wait_send()
        return carry

    def drain_links(i, carry):
        for o in (1, 2, 3):
            dest = lax.rem(x + o, 4)
            x_copy(i, o, 2 * dest + i, x).wait_send()
            s_copy(i, o, dest, x).wait_send()

        @pl.when(y != 2 * c + i)
        def _():
            y_copy(i, y, 2 * c + i).wait_send()

        return carry

    lax.fori_loop(0, 8, drain, 0)
    lax.fori_loop(0, 2, drain_links, 0)

    @pl.when(is_root)
    def _():
        for o in (1, 2, 3):
            dest = lax.rem(y + o, 4)
            u_copy(i_root, o, dest).wait_send()

            @pl.when(dest > 0)
            def _():
                p_copy(i_root, o, dest).wait_send()

        @pl.when(z < 2)
        def _():
            z_next(z_out).wait_send()

        @pl.when(z == 1)
        def _():
            z_skip().wait_send()

        @pl.when(z == 2)
        def _():
            line_copy().wait_send()


def shards(queries, keys, values, betas, gate, norm_gain):
    here = pl.BlockSpec(memory_space=pltpu.VMEM)
    outside = pl.BlockSpec(memory_space=pl.ANY)
    vm = pltpu.VMEM
    dma = pltpu.SemaphoreType.DMA
    tile = (DK, DK)
    normed = pl.pallas_call(
        layer_kernel,
        in_specs=[outside] * 3 + [here] * 2,
        out_specs=here,
        out_shape=jax.ShapeDtypeStruct((CT, H * DK), bf16),
        scratch_shapes=[
            vm((CT, H * DK), bf16),
            vm((CT, 2, H * DK), bf16),
            vm((CT, 2, H * DK), bf16),
            vm((H, STEPS), f32),
            vm((LEVELS - 1, HALF, HALF), bf16),
            vm((H, 4) + tile, bf16),
            vm((3, 8, 4) + tile, bf16),
            vm((8, 3) + tile, bf16),
            vm((4, 2, 3) + tile, bf16),
            vm((2, 4, 2) + tile, bf16),
            vm((2, 4) + tile, f32),
            vm((2, 3) + tile, bf16),
            vm((4, 3) + tile, bf16),
            vm((4, 4) + tile, bf16),
            vm((2, 4) + tile, bf16),
            vm((4,) + tile, bf16),
            vm((4,) + tile, bf16),
            vm(tile, bf16),
            vm(tile, bf16),
            vm(tile, bf16),
            vm((2,) + tile, bf16),
            vm((4, 2) + tile, bf16),
            vm((8,) + tile, bf16),
            vm((8,) + tile, bf16),
            vm((8,) + tile, bf16),
            vm((8,) + tile, bf16),
            dma((8,)),
            dma((8,)),
            dma((4, 2)),
            dma((4, 2)),
            dma((2,)),
            dma((4,)),
            dma((3,)),
            dma((3,)),
            dma((4,)),
            dma((2,)),
            dma((4,)),
            dma((2,)),
            dma((4, 2)),
            dma((8,)),
            dma((8,)),
            dma((8,)),
            dma((1,)),
            dma((H,)),
            dma((H,)),
        ],
        compiler_params=pltpu.CompilerParams(
            collective_id=0, has_side_effects=True, vmem_limit_bytes=60 << 20
        ),
    )(queries, keys, values, betas.transpose(1, 2, 0), norm_gain.reshape(1, DK))
    gate = gate.astype(f32)
    return (normed.astype(f32) * (gate / (1.0 + jnp.exp(-gate)))).astype(bf16)


def solution(mesh):
    torus = Mesh(mesh.devices.reshape(4, 4, 4, 2), AXES)
    rows, pairs = P(AXES, None), P(AXES, None, None)
    return jax.shard_map(
        shards, mesh=torus, in_specs=(rows, pairs, pairs, pairs, rows, P()), out_specs=rows, check_vma=False
    )
```

```python
import functools

import jax
import jax.numpy as jnp
from jax import lax
from jax.experimental import pallas as pl
from jax.experimental.pallas import tpu as pltpu
from jax.sharding import Mesh
from jax.sharding import PartitionSpec as P

H = 16
DK = 256
CT = 128
STEPS = 256
EPS = 1e-06
LEVELS = 8
HALF = 128
f32 = jnp.float32
bf16 = jnp.bfloat16
AXES = ("z", "y", "x", "core")
MESH = pl.DeviceIdType.MESH


def mm(a, b, dims=((1,), (0,))):
    return lax.dot_general(a, b, (dims, ((), ())), preferred_element_type=f32)


def split(x):
    hi = x.astype(bf16)
    return hi, (x - hi.astype(f32)).astype(bf16)


def mm_right(a, b):
    hi, lo = b
    return mm(a, hi) + mm(a, lo)


def mm_both(a, b):
    return mm(a[0], b[0]) + (mm(a[0], b[1]) + mm(a[1], b[0]))


def factors(ks, vs, beta_rows, mask_ref):
    row = lax.broadcasted_iota(jnp.int32, (STEPS, STEPS), 0)
    col = lax.broadcasted_iota(jnp.int32, (STEPS, STEPS), 1)
    eye = row == col
    eye_h = eye[:HALF, :HALF]
    n = range(len(ks))
    both = range(2)
    part = (slice(0, HALF), slice(HALF, STEPS))
    gram = [mm(k, k, ((1,), (1,))) for k in ks]
    g = [jnp.sum(jnp.where(eye, x, 0.0), axis=0, keepdims=True) + EPS for x in gram]
    c = [beta_rows[i] / g[i] for i in n]
    low = [split(jnp.where(row > col, x, 0.0)) for x in gram]
    tau = [[jnp.where(eye_h, c[i][:, part[j]], 0.0) for j in both] for i in n]
    diag = [[low[i][0][part[j], part[j]] for j in both] for i in n]
    for level in range(LEVELS - 1):
        edge = [[x * mask_ref[level] for x in d] for d in diag]
        tb = [[x.astype(bf16) for x in t] for t in tau]
        if level == 0:
            step = [
                [(edge[i][j].astype(f32) * c[i][:, part[j]]).astype(bf16) for j in both] for i in n
            ]
        else:
            step = [[mm(edge[i][j], tb[i][j]).astype(bf16) for j in both] for i in n]
        tau = [[tau[i][j] - mm(tb[i][j], step[i][j]) for j in both] for i in n]
    tb = [[x.astype(bf16) for x in t] for t in tau]
    step = [mm(low[i][0][part[1], part[0]], tb[i][0]).astype(bf16) for i in n]
    below = [-mm(tb[i][1], step[i]) for i in n]
    zero = jnp.zeros((HALF, HALF), bf16)
    tb = [
        jnp.concatenate(
            [
                jnp.concatenate([tb[i][0], zero], axis=1),
                jnp.concatenate([below[i].astype(bf16), tb[i][1]], axis=1),
            ],
            axis=0,
        )
        for i in n
    ]
    t32 = [x.astype(f32) for x in tb]
    rest = [
        jnp.where(eye, 1.0, 0.0) - t32[i] * (g[i] / beta_rows[i]) - mm_right(tb[i], low[i]) for i in n
    ]
    tau = [t32[i] + mm(rest[i].astype(bf16), tb[i]) for i in n]
    ts = [split(x) for x in tau]
    w = [split(mm(ts[i][0], ks[i]) + mm(ts[i][1], ks[i])) for i in n]
    ts = [split(tau[i] * jnp.sqrt(g[i])) for i in n]
    y = [split(mm(ts[i][0], vs[i]) + mm(ts[i][1], vs[i])) for i in n]
    kt = [k.T for k in ks]
    a = [jnp.where(eye, 1.0, 0.0) - mm_right(kt[i], w[i]) for i in n]
    b = [mm_right(kt[i], y[i]) for i in n]
    return a, b, w, y


def answers(ks, qs, w, y):
    n = range(len(ks))
    token = lax.broadcasted_iota(jnp.int32, (CT, STEPS), 0)
    step_of = lax.broadcasted_iota(jnp.int32, (CT, STEPS), 1)
    causal = step_of // 2 <= token
    p = [split(jnp.where(causal, mm(qs[i], ks[i], ((1,), (1,))), 0.0)) for i in n]
    q32 = [q.astype(f32) for q in qs]
    unit = [lax.rsqrt(jnp.sum(q * q, axis=-1, keepdims=True) + EPS) for q in q32]
    qt = [(q32[i] - mm_both(p[i], w[i])) * unit[i] for i in n]
    ot = [mm_both(p[i], y[i]) * unit[i] for i in n]
    return qt, ot


def make_masks(mask_ref):
    row = lax.broadcasted_iota(jnp.int32, (HALF, HALF), 0)
    col = lax.broadcasted_iota(jnp.int32, (HALF, HALF), 1)
    differ = jnp.bitwise_xor(row, col)
    for level in range(LEVELS - 1):
        inside = (differ >= (1 << level)) & (differ < (2 << level))
        mask_ref[level] = jnp.where(inside, 1.0, 0.0).astype(bf16)


def put_pair(ref, values):
    ref[0], ref[1] = split(values)


def layer_kernel(
    q_hbm, k_hbm, v_hbm, beta_ref, gain_ref, out_ref,
    q_ref, k_ref, v_ref, beta, mask, wy, blk, x_out, x_in, pxa, pxb, y_out, y_in, pf_out, pf_in, line, line_in,
    z_in, z_mid, z_out, u_in,
    s_out, s_in, c_out, c_in,
    core_send, core_recv, x_send, x_recv, y_send, y_recv, z_send, z_recv, p_send, p_recv, u_send, u_recv, s_send, s_recv,
    c_send, c_recv, q_here, k_here, v_here,
):
    z, y, x, c = (lax.axis_index(name) for name in AXES)
    other = {"core": 1 - c}

    def along(axis, index, offset):
        return {axis: lax.rem(index + offset, 4)}

    barrier = pltpu.get_barrier_semaphore()
    greeted = [other] + [along("x", x, o) for o in (1, 2, 3)] + [along("y", y, o) for o in (1, 2, 3)]
    greeted += [along("z", z, o) for o in (1, 2, 3)]
    for device in greeted:
        pl.semaphore_signal(barrier, inc=1, device_id=device, device_id_type=MESH)

    def remote(src, dst, send, recv, device):
        return pltpu.make_async_remote_copy(
            src_ref=src, dst_ref=dst, send_sem=send, recv_sem=recv, device_id=device, device_id_type=MESH
        )

    def core_copy(j, slot):
        return remote(blk.at[2, j], blk.at[slot, j], core_send.at[j], core_recv.at[j], other)

    def x_copy(i, o, j, source):
        return remote(
            x_out.at[j], x_in.at[source, i], x_send.at[o, i], x_recv.at[source, i], along("x", x, o)
        )

    def y_copy(i, source, root):
        return remote(y_out.at[i], y_in.at[source], y_send.at[i], y_recv.at[source], {"y": root})

    def z_next(source):
        return remote(source, z_in, z_send.at[0], z_recv.at[0], along("z", z, 1))

    def z_skip():
        return remote(z_out, z_mid, z_send.at[1], z_recv.at[1], along("z", z, 2))

    def line_copy():
        return remote(line, line_in, z_send.at[2], z_recv.at[2], along("z", z, 1))

    def p_copy(i, o, dest):
        return remote(pf_out.at[dest], pf_in.at[i], p_send.at[o], p_recv.at[i], {"y": dest})

    def u_copy(i, o, dest):
        return remote(z_in, u_in.at[i], u_send.at[o], u_recv.at[i], {"y": dest})

    def s_copy(i, o, dest, source):
        j = 2 * source + i
        return remote(s_out.at[dest, i], s_in.at[j], s_send.at[o, i], s_recv.at[j], along("x", x, o))

    def c_copy(j):
        return remote(c_out.at[j], c_in.at[j], c_send.at[j], c_recv.at[j], other)

    def lanes_of(head):
        return pl.ds(pl.multiple_of(head * DK, DK), DK)

    def load(head):
        lanes = lanes_of(head)
        return (
            pltpu.make_async_copy(k_hbm.at[:, :, lanes], k_ref.at[:, :, lanes], k_here.at[head]),
            pltpu.make_async_copy(v_hbm.at[:, :, lanes], v_ref.at[:, :, lanes], v_here.at[head]),
        )

    def place(own, j):
        return own * c + (1 - own) * 2, 8 * (own * c + (1 - own) * (1 - c)) + j

    def away(p):
        own = p % 2
        return [(own, 2 * lax.rem(x + o, 4) + p // 2) for o in (1, 3, 2)]

    near = [(own, 2 * x + i) for own in (0, 1) for i in (0, 1)]

    def start_loads(group):
        for own, j in group:
            for copy in load(place(own, j)[1]):
                copy.start()

    def loads_of(p, carry):
        start_loads(away(p))
        return carry

    lax.fori_loop(0, 2, loads_of, 0)
    start_loads(near)
    lax.fori_loop(2, 4, loads_of, 0)
    q_load = pltpu.make_async_copy(q_hbm, q_ref, q_here.at[0])
    q_load.start()

    make_masks(mask)
    token = lax.broadcasted_iota(jnp.int32, (CT, STEPS), 0)
    step_of = lax.broadcasted_iota(jnp.int32, (CT, STEPS), 1)
    spread = [jnp.where(step_of == 2 * token + r, 1.0, 0.0).astype(bf16) for r in (0, 1)]
    beta[...] = mm(beta_ref[0], spread[0]) + mm(beta_ref[1], spread[1])

    def make_pairs(group):
        places = [place(own, j) for own, j in group]
        for slot, head in places:
            for copy in load(head):
                copy.wait()
        lanes = [lanes_of(head) for slot, head in places]
        a, b, w, y_rows = factors(
            [k_ref[:, :, n].reshape(STEPS, DK) for n in lanes],
            [v_ref[:, :, n].reshape(STEPS, DK) for n in lanes],
            [beta[pl.ds(head, 1), :] for slot, head in places],
            mask,
        )
        for n, (slot, head) in enumerate(places):
            j = group[n][1]
            put_pair(blk.at[slot, j, pl.ds(0, 2)], a[n])
            put_pair(blk.at[slot, j, pl.ds(2, 2)], b[n])
            wy[head, 0], wy[head, 1] = w[n]
            wy[head, 2], wy[head, 3] = y_rows[n]

    def merge(j, pair):
        core_copy(j, 1 - c).wait_recv()
        later = (blk[1, j, 0], blk[1, j, 1])
        put_pair(pair.at[pl.ds(0, 2)], mm_both(later, (blk[0, j, 0], blk[0, j, 1])))
        pair[2] = (
            mm_both(later, (blk[0, j, 2], blk[0, j, 3]))
            + blk[1, j, 2].astype(f32)
            + blk[1, j, 3].astype(f32)
        ).astype(bf16)

    def phase(p, carry):
        i = p // 2
        group = away(p)
        make_pairs(group)

        @pl.when(p == 0)
        def _():
            pl.semaphore_wait(barrier, len(greeted))

        @pl.when(p % 2 == 0)
        def _():
            for own, j in group:
                core_copy(j, c).start()

        @pl.when(p % 2 == 1)
        def _():
            for o in (1, 3, 2):
                j = 2 * lax.rem(x + o, 4) + i
                merge(j, x_out.at[j])
                x_copy(i, o, j, x).start()

        @pl.when(p == 1)
        def _():
            make_pairs(near)
            for i in (0, 1):
                core_copy(2 * x + i, c).start()

        return carry

    lax.fori_loop(0, 4, phase, 0)
    for i in (0, 1):
        merge(2 * x + i, x_in.at[x, i])

    def answer(p, carry):
        heads = [4 * p + n for n in range(4)]
        lanes = [lanes_of(h) for h in heads]
        q_now, o_now = answers(
            [k_ref[:, :, n].reshape(STEPS, DK) for n in lanes],
            [q_ref[:, n] for n in lanes],
            [(wy[h, 0], wy[h, 1]) for h in heads],
            [(wy[h, 2], wy[h, 3]) for h in heads],
        )
        for n in range(4):
            h = heads[n]
            wy[h, 0, :CT], wy[h, 0, CT:] = split(q_now[n])
            wy[h, 1, :CT], wy[h, 1, CT:] = split(o_now[n])
        return carry


    def compose(pairs, whole, prefix):
        p = [(pairs[n, 0], pairs[n, 1]) for n in range(4)]
        b = [pairs[n, 2] for n in range(4)]
        a10, a32 = split(mm_both(p[1], p[0])), split(mm_both(p[3], p[2]))
        b10 = mm(p[1][0], b[0]) + mm(p[1][1], b[0]) + b[1].astype(f32)
        b32 = mm(p[3][0], b[2]) + mm(p[3][1], b[2]) + b[3].astype(f32)
        b10s = split(b10)
        whole(split(mm_both(a32, a10)), mm_both(a32, b10s) + b32)
        prefix(1, p[0], b[0].astype(f32))
        prefix(2, a10, b10)
        prefix(3, split(mm_both(p[2], a10)), mm_both(p[2], b10s) + b[2].astype(f32))

    def identity():
        eye = lax.broadcasted_iota(jnp.int32, (DK, DK), 0) == lax.broadcasted_iota(jnp.int32, (DK, DK), 1)
        return jnp.where(eye, 1.0, 0.0).astype(bf16), jnp.zeros((DK, DK), bf16)

    for i in (0, 1):
        pxa[i, 0, 0], pxa[i, 0, 1] = identity()
        pxb[i, 0] = jnp.zeros((DK, DK), f32)

    def over_x(i):
        for o in (1, 3, 2):
            source = lax.rem(x + o, 4)
            x_copy(i, o, 2 * source + i, source).wait_recv()
        root = 2 * c + i

        def whole(a, b):
            @pl.when(y == root)
            def _():
                y_in[y, 0], y_in[y, 1] = a
                y_in[y, 2] = b.astype(bf16)

            @pl.when(y != root)
            def _():
                y_out[i, 0], y_out[i, 1] = a
                y_out[i, 2] = b.astype(bf16)
                y_copy(i, y, root).start()

        def prefix(n, a, b):
            pxa[i, n, 0], pxa[i, n, 1] = a
            pxb[i, n] = b

        compose(x_in.at[:, i], whole, prefix)

    i_root = y % 2
    is_root = y // 2 == c

    def over_y():
        for o in (1, 3, 2):
            y_copy(i_root, lax.rem(y + o, 4), y).wait_recv()

        def whole(a, b):
            line[0], line[1] = a
            line[2], line[3] = split(b)

            @pl.when(z == 0)
            def _():
                z_next(line.at[2]).start()

            @pl.when(z == 2)
            def _():
                line_copy().start()

        def prefix(n, a, b):
            pf_out[n, 0], pf_out[n, 1] = a
            pf_out[n, 2], pf_out[n, 3] = split(b)

        compose(y_in, whole, prefix)
        for o in (1, 2, 3):
            dest = lax.rem(y + o, 4)

            @pl.when(dest > 0)
            def _():
                p_copy(i_root, o, dest).start()

        @pl.when(y > 0)
        def _():
            for n in range(4):
                pf_in[i_root, n] = pf_out[y, n]

    def advance(pair, s):
        out = mm(pair[0], s) + mm(pair[1], s)
        return out + pair[2].astype(f32) + pair[3].astype(f32)

    def over_z():
        @pl.when(z == 0)
        def _():
            z_in[...] = jnp.zeros((DK, DK), bf16)

        @pl.when(z == 1)
        def _():
            z_next(z_out).wait_recv()
            z_out[...] = advance(line, z_in[...]).astype(bf16)
            z_skip().start()
            z_next(z_out).start()

        @pl.when(z == 2)
        def _():
            z_next(z_out).wait_recv()

        @pl.when(z == 3)
        def _():
            line_copy().wait_recv()
            z_skip().wait_recv()
            z_in[...] = advance(line_in, z_mid[...]).astype(bf16)

        for o in (2, 1, 3):
            u_copy(i_root, o, lax.rem(y + o, 4)).start()
        u_in[i_root] = z_in[...]

    def down(i):
        root = 2 * c + i

        @pl.when(y == 0)
        def _():
            pf_in[i, 0], pf_in[i, 1] = identity()
            pf_in[i, 2] = jnp.zeros((DK, DK), bf16)
            pf_in[i, 3] = jnp.zeros((DK, DK), bf16)

        @pl.when((y != root) & (y > 0))
        def _():
            p_copy(i, 1, y).wait_recv()

        @pl.when(y != root)
        def _():
            u_copy(i, 1, y).wait_recv()

        s = split(advance(pf_in.at[i], u_in[i]))
        for o in (1, 3, 2, 0):
            dest = lax.rem(x + o, 4)
            now = (mm_both((pxa[i, dest, 0], pxa[i, dest, 1]), s) + pxb[i, dest]).astype(bf16)
            if o:
                s_out[dest, i] = now
                s_copy(i, o, dest, x).start()
            else:
                s_in[2 * x + i] = now

    first_root = is_root & (i_root == 0)
    second_root = is_root & (i_root == 1)
    over_x(0)
    q_load.wait()
    lax.fori_loop(0, 4, answer, 0)
    pl.when(first_root)(over_y)
    over_x(1)
    pl.when(first_root)(over_z)
    pl.when(second_root)(over_y)
    pl.when(second_root & (z < 2))(over_z)
    down(0)
    pl.when(second_root & (z >= 2))(over_z)
    down(1)

    def over_cores(i):
        for o in (0, 1, 3, 2):
            source = lax.rem(x + o, 4)
            j = 2 * source + i
            if o:
                s_copy(i, o, source, source).wait_recv()
            first = s_in[j]
            second = advance(blk.at[0, j], first).astype(bf16)
            c_out[j] = jnp.where(c == 0, second, first)
            c_copy(j).start()
            s_in[j] = jnp.where(c == 0, first, second)

    def finish(heads, states):
        o = [mm(wy[h, 0, :CT], s) + mm(wy[h, 0, CT:], s) for h, s in zip(heads, states)]
        o = [x + wy[h, 1, :CT].astype(f32) + wy[h, 1, CT:].astype(f32) for h, x in zip(heads, o)]
        scale = [lax.rsqrt(jnp.mean(x * x, axis=-1, keepdims=True) + EPS) for x in o]
        for n, h in enumerate(heads):
            out_ref[:, lanes_of(h)] = (o[n] * scale[n] * gain_ref[...]).astype(bf16)

    for i in (0, 1):
        over_cores(i)
        js = [2 * n + i for n in range(4)]
        finish([8 * c + j for j in js], [s_in[j] for j in js])
        for j in js:
            c_copy(j).wait_recv()
        finish([8 * (1 - c) + j for j in js], [c_in[j] for j in js])

    def drain(j, carry):
        core_copy(j, c).wait_send()
        c_copy(j).wait_send()
        return carry

    def drain_links(i, carry):
        for o in (1, 2, 3):
            dest = lax.rem(x + o, 4)
            x_copy(i, o, 2 * dest + i, x).wait_send()
            s_copy(i, o, dest, x).wait_send()

        @pl.when(y != 2 * c + i)
        def _():
            y_copy(i, y, 2 * c + i).wait_send()

        return carry

    lax.fori_loop(0, 8, drain, 0)
    lax.fori_loop(0, 2, drain_links, 0)

    @pl.when(is_root)
    def _():
        for o in (1, 2, 3):
            dest = lax.rem(y + o, 4)
            u_copy(i_root, o, dest).wait_send()

            @pl.when(dest > 0)
            def _():
                p_copy(i_root, o, dest).wait_send()

        @pl.when(z < 2)
        def _():
            z_next(z_out).wait_send()

        @pl.when(z == 1)
        def _():
            z_skip().wait_send()

        @pl.when(z == 2)
        def _():
            line_copy().wait_send()


def shards(queries, keys, values, betas, gate, norm_gain):
    here = pl.BlockSpec(memory_space=pltpu.VMEM)
    outside = pl.BlockSpec(memory_space=pl.ANY)
    vm = pltpu.VMEM
    dma = pltpu.SemaphoreType.DMA
    tile = (DK, DK)
    normed = pl.pallas_call(
        layer_kernel,
        in_specs=[outside] * 3 + [here] * 2,
        out_specs=here,
        out_shape=jax.ShapeDtypeStruct((CT, H * DK), bf16),
        scratch_shapes=[
            vm((CT, H * DK), bf16),
            vm((CT, 2, H * DK), bf16),
            vm((CT, 2, H * DK), bf16),
            vm((H, STEPS), f32),
            vm((LEVELS - 1, HALF, HALF), bf16),
            vm((H, 4) + tile, bf16),
            vm((3, 8, 4) + tile, bf16),
            vm((8, 3) + tile, bf16),
            vm((4, 2, 3) + tile, bf16),
            vm((2, 4, 2) + tile, bf16),
            vm((2, 4) + tile, f32),
            vm((2, 3) + tile, bf16),
            vm((4, 3) + tile, bf16),
            vm((4, 4) + tile, bf16),
            vm((2, 4) + tile, bf16),
            vm((4,) + tile, bf16),
            vm((4,) + tile, bf16),
            vm(tile, bf16),
            vm(tile, bf16),
            vm(tile, bf16),
            vm((2,) + tile, bf16),
            vm((4, 2) + tile, bf16),
            vm((8,) + tile, bf16),
            vm((8,) + tile, bf16),
            vm((8,) + tile, bf16),
            dma((8,)),
            dma((8,)),
            dma((4, 2)),
            dma((4, 2)),
            dma((2,)),
            dma((4,)),
            dma((3,)),
            dma((3,)),
            dma((4,)),
            dma((2,)),
            dma((4,)),
            dma((2,)),
            dma((4, 2)),
            dma((8,)),
            dma((8,)),
            dma((8,)),
            dma((1,)),
            dma((H,)),
            dma((H,)),
        ],
        compiler_params=pltpu.CompilerParams(
            collective_id=0, has_side_effects=True, vmem_limit_bytes=63 << 20
        ),
    )(queries, keys, values, betas.transpose(1, 2, 0), norm_gain.reshape(1, DK))
    gate = gate.astype(f32)
    return (normed.astype(f32) * (gate / (1.0 + jnp.exp(-gate)))).astype(bf16)


def solution(mesh):
    torus = Mesh(mesh.devices.reshape(4, 4, 4, 2), AXES)
    rows, pairs = P(AXES, None), P(AXES, None, None)
    return jax.shard_map(
        shards, mesh=torus, in_specs=(rows, pairs, pairs, pairs, rows, P()), out_specs=rows, check_vma=False
    )
```
